32 devices in a mesh: dp: 8 (over z, y), mp: 4 (over x, core).
Axes of the slice: x: 2, y: 2, z: 4, core: 2. Of those that a mesh axis runs over, the one named last changes fastest.
Arguments:
- pre_act: bfloat16 [1024, 36864], P('dp', 'mp'), may hold values from -6 to 6
- grad_out: bfloat16 [1024, 18432], P('dp', 'mp'), may hold values from -6 to 6
- row_state: float32 [4, 4608], P(None, 'dp'), may hold values from 3e-05 to 0.0003
- col_state: float32 [36864], P('mp'), may hold values from 3e-05 to 0.0003
Outputs:
- update: bfloat16 [4, 4608, 36864], P(None, 'dp', 'mp')
- row_new: float32 [4, 4608], P(None, 'dp')
- col_new: float32 [36864], P('mp')
The draws below stay inside these ranges and needn't reach their ends.
All inputs are finite; a program needn't handle non-finite values.
Results may differ from the reference program's by a relative error of at most 0.0015.
The reference program's roundings to bfloat16 on the way (of `hidden`) count: a program that leaves them out, or rounds other values in their place, can miss the bound.
Values may be sent and summed in bfloat16 or wider, within the bound.
A program may use at most 192 MiB of HBM per device.

```python
import math
import jax
import jax.numpy as jnp
from jax import lax

D = 18432
FFW = 36864
TOKENS = 1024
N_MP = 4


def raised(array, rng, source, target, shards_of, factor):
    def block_of(position):
        return (jnp.arange(array.shape[position]) // (array.shape[position] // shards_of)).reshape((-1,) + (1,) * (array.ndim - 1 - position))

    near = jax.random.permutation(rng, shards_of)[block_of(target)]
    other_side = (block_of(target) + shards_of // 2) % shards_of
    return jnp.where((block_of(source) == near) | (block_of(source) == other_side), factor * array, array)


def level_of(key, dims, shards, smallest, top_value):
    def one(dim, shards_of):
        steps = jax.random.uniform(jax.random.fold_in(jax.random.fold_in(key, 6), dim), (shards_of,), jnp.float32, smallest / len(shards), top_value / len(shards))
        return jnp.repeat(jnp.exp(steps), dims[dim] // shards_of).reshape((-1,) + (1,) * (len(dims) - dim - 1))

    factor_of = one(*shards[0])
    for cut in shards[1:]:
        factor_of = factor_of * one(*cut)
    return factor_of


def normal_values(rng, extent, spread, reach, split=(), dtype=jnp.bfloat16):
    level = level_of(rng, extent, split, -0.22, 0.18) if split else 1.0
    entries = jax.random.normal(rng, extent, jnp.float32) * spread * level
    return jnp.minimum(jnp.maximum(entries, -reach), reach).astype(dtype)


def gaussian_with(key, shape, scale, bound, cuts, heavy, kind=jnp.bfloat16):
    result = scale * jax.random.normal(key, shape, jnp.float32)
    if cuts:
        result = result * level_of(key, shape, cuts, -0.22, 0.18)
    return jnp.clip(raised(result, jax.random.fold_in(key, 3), *heavy), -bound, bound).astype(kind)


def setup_inputs(seed: int = 0) -> dict:
    key_of = jax.random.split(jax.random.key(seed), 5)
    pre_act = normal_values(key_of[0], (TOKENS, FFW), 1.0, 6.0, ((0, 8), (1, 4)))
    grad_out = gaussian_with(key_of[1], (TOKENS, D), 1.0, 6.0, ((0, 8), (1, 4)), (0, 1, 8, 2.0))
    row_state = jnp.clip(jnp.exp(math.log(0.0003) - 2.3025852 * jax.random.uniform(key_of[2], (N_MP, D // N_MP), jnp.float32) ** level_of(key_of[2], (N_MP, D // N_MP), ((1, 8),), -0.2, 0.2)), 2.9999999242136255e-05, 0.0003)
    col_state = jnp.clip(jnp.exp(math.log(0.0003) - 2.3025852 * jax.random.uniform(key_of[3], (FFW,), jnp.float32) ** level_of(key_of[3], (FFW,), ((0, 4),), -0.2, 0.2)), 2.9999999242136255e-05, 0.0003)
    return dict(pre_act=pre_act, grad_out=grad_out, row_state=row_state, col_state=col_state)


decay = 1.0 - 2.0 ** (-0.8)
tiny = 1e-30

def reference(pre_act, grad_out, row_state, col_state):
    hidden = jax.nn.gelu(pre_act.astype(jnp.float32)).astype(jnp.bfloat16)
    grad = jnp.dot(grad_out.T, hidden, preferred_element_type=jnp.float32) / TOKENS
    row_sum = lax.optimization_barrier(jnp.sum(grad * grad, axis=1))
    col_sum = lax.optimization_barrier(jnp.sum(grad * grad, axis=0))
    row_flat = row_state.reshape(D)
    row_new = decay * row_flat + (1.0 - decay) * (row_sum / FFW + tiny)
    col_new = decay * col_state + (1.0 - decay) * (col_sum / D + tiny)
    scale = jnp.mean(row_new)
    update = (grad * lax.rsqrt(row_new[:, None] * col_new[None, :] / scale)).astype(jnp.bfloat16)
    return (update.reshape(N_MP, D // N_MP, FFW), row_new.reshape(N_MP, D // N_MP), col_new)
```

```python
import functools

import jax
import jax.numpy as jnp
from jax import lax
from jax.experimental import pallas as pl
from jax.experimental.pallas import tpu as pltpu
from jax.sharding import PartitionSpec as P

D = 18432
MESH = pl.DeviceIdType.MESH
VMEM = pltpu.VMEM

decay = 1.0 - 2.0 ** (-0.8)
tiny = 1e-30

PIECES = 18
G_SEND_STEP = 2
G_READY_STEP = 8


def gather_kernel(
    dp_count, mp_count, pieces,
    pre_ref, g_ref, row_ref, col_ref,
    hid_out, gt_out, row_new, col_new, scale_out,
    hid, gt, row_acc, row_part, col_part, total_part,
    up_sem, down_sem, side_sem, recv_sem,
    g_local, g_send, g_recv, m_send, m_recv,
    out_sem, gt_sem, r_send, r_recv, c_send, c_recv, t_send, t_recv,
):
    rows = pre_ref.shape[0]
    width = hid.shape[2]
    depth = dp_count // 2
    slice_width = gt.shape[1]
    tokens = rows * dp_count
    d = lax.axis_index("dp")
    a = lax.axis_index("mp")
    z = d // 2
    y = d % 2
    period = 2 * max(depth - 1, 1)

    def peer(i):
        return lax.rem(d + i, dp_count)

    def mate(j):
        return lax.rem(a + j, mp_count)

    barrier = pltpu.get_barrier_semaphore()
    for i in range(1, dp_count):
        pl.semaphore_signal(barrier, inc=1, device_id=(peer(i), a), device_id_type=MESH)
    for j in range(1, mp_count):
        pl.semaphore_signal(barrier, inc=1, device_id=(d, mate(j)), device_id_type=MESH)
    pl.semaphore_wait(barrier, dp_count + mp_count - 2)

    def remote(src, dst, send, recv, device):
        return pltpu.make_async_remote_copy(
            src_ref=src, dst_ref=dst, send_sem=send, recv_sem=recv,
            device_id=device, device_id_type=MESH,
        )

    def tok(dev):
        return pl.ds(pl.multiple_of(dev * rows, rows), rows)

    own_g = pltpu.make_async_copy(g_ref.at[d], gt.at[a, :, tok(d)], g_local)
    own_g.start()
    for i in range(1, dp_count):
        remote(g_ref.at[peer(i)], gt.at[a, :, tok(d)], g_send.at[i], g_recv.at[i], (peer(i), a)).start()

    def spread_g():
        own_g.wait()
        for i in range(1, dp_count):
            src = lax.rem(d - i + dp_count, dp_count)
            block = gt.at[a, :, tok(src)]
            remote(block, block, g_send.at[i], g_recv.at[i], (peer(i), a)).wait_recv()
        for j in range(1, mp_count):
            remote(gt.at[a], gt.at[a], m_send.at[j], m_recv.at[j], (d, mate(j))).start()

    def finish_g():
        for j in range(1, mp_count):
            src = lax.rem(a - j + mp_count, mp_count)
            remote(gt.at[src], gt.at[src], m_send.at[j], m_recv.at[j], (d, mate(j))).wait_recv()
        pltpu.make_async_copy(gt, gt_out, gt_sem).start()

    def block_of(src, p):
        return hid.at[p, tok(src)]

    def arrive(src, p):
        block = block_of(src, p)
        remote(block, block, side_sem.at[src, p], recv_sem.at[src, p], (d, a)).wait_recv()

    def side_first(p):
        return lax.rem(p, period) == min(2, period - 1)

    def push(go, src, p, up, down, side):
        block = block_of(src, p)
        for wanted, sem, dev in ((up, up_sem, d + 2), (down, down_sem, d - 2), (side, side_sem, z * 2 + 1 - y)):
            if wanted is None:
                continue

            @pl.when(wanted)
            def _(sem=sem, dev=dev):
                copy = remote(block, block, sem.at[src, p], recv_sem.at[src, p], (dev, a))
                if go:
                    copy.start()
                else:
                    copy.wait_send()

    up_ok = z + 1 < depth
    down_ok = z > 0
    always = z >= 0

    def events(t, go):
        @pl.when(t < pieces)
        def _():
            if go:
                cols = pl.ds(pl.multiple_of(t * width, width), width)
                part = jax.nn.gelu(pre_ref[:, cols].astype(jnp.float32)).astype(jnp.bfloat16)
                hid[t, tok(d), :] = part
            push(go, d, t, up_ok, down_ok, always)

        def passing(zs, ys, p, valid, up, down, side):
            @pl.when(valid)
            def _():
                src = zs * 2 + ys
                if go:
                    arrive(src, p)
                push(go, src, p, up, down, side)

        for k in range(1, depth):
            p = t - k
            live = (p >= 0) & (p < pieces)
            row_first = jnp.logical_not(side_first(p))
            passing(z - k, y, p, live & (z - k >= 0), up_ok, None, row_first)
            passing(z + k, y, p, live & (z + k < depth), None, down_ok, row_first)
        for k in range(depth):
            p = t - k - 1
            live = (p >= 0) & (p < pieces) & side_first(p)
            if k == 0:
                passing(z, 1 - y, p, live, up_ok, down_ok, None)
            else:
                passing(z - k, 1 - y, p, live & (z - k >= 0), up_ok, None, None)
                passing(z + k, 1 - y, p, live & (z + k < depth), None, down_ok, None)

    row_acc[...] = jnp.zeros_like(row_acc)

    def work(c):
        @pl.when(jnp.logical_not(side_first(c)))
        def _():
            for zs in range(depth):
                arrive(zs * 2 + 1 - y, c)

        pltpu.make_async_copy(hid.at[c], hid_out.at[c], out_sem.at[c]).start()
        block = hid[c]

        def one(m, col):
            prod = jnp.dot(gt[m], block, preferred_element_type=jnp.float32)
            sq = prod * prod
            part = sq[:, 0:128]
            for q in range(1, width // 128):
                part = part + sq[:, q * 128:(q + 1) * 128]
            row_acc[m] += part
            return col + jnp.sum(sq, axis=0, keepdims=True)

        col = lax.fori_loop(0, mp_count, one, jnp.zeros((1, width), jnp.float32))
        col_part[d, pl.ds(c, 1), :] = col

    def done_by(t):
        return jnp.clip(jnp.minimum(2 * (t - G_READY_STEP + 1), t - depth + 1), 0, pieces)

    steps = pieces + depth

    @pl.loop(0, steps)
    def _(t):
        events(t, True)

        @pl.when(t == G_SEND_STEP)
        def _():
            spread_g()

        @pl.when(t == G_READY_STEP)
        def _():
            finish_g()

        @pl.loop(done_by(t - 1), done_by(t))
        def _(c):
            work(c)

    ones = jnp.ones((8, 128), jnp.float32)
    for m in range(mp_count):
        turned = lax.dot_general(
            ones, row_acc[m], (((1,), (1,)), ((), ())),
            precision=lax.Precision.HIGHEST, preferred_element_type=jnp.float32,
        )
        row_part[a, m:m + 1, :] = turned[0:1]
    for j in range(1, mp_count):
        remote(row_part.at[a], row_part.at[a], r_send.at[j], r_recv.at[j], (d, mate(j))).start()
    for i in range(1, dp_count):
        remote(col_part.at[d], col_part.at[d], c_send.at[i], c_recv.at[i], (peer(i), a)).start()

    for j in range(1, mp_count):
        src = lax.rem(a - j + mp_count, mp_count)
        remote(row_part.at[src], row_part.at[src], r_send.at[j], r_recv.at[j], (d, mate(j))).wait_recv()
    inv = 1.0 / (tokens * tokens)
    all_hidden = pieces * width * mp_count
    row_sum = row_part[0]
    for m in range(1, mp_count):
        row_sum = row_sum + row_part[m]
    new = decay * row_ref[...] + (1.0 - decay) * (row_sum * inv / all_hidden + tiny)
    row_new[...] = new
    own_total = jnp.sum(jnp.sum(new, axis=1, keepdims=True), axis=0, keepdims=True)
    total_part[d] = jnp.broadcast_to(own_total, (8, 128))
    for i in range(1, dp_count):
        remote(total_part.at[d], total_part.at[d], t_send.at[i], t_recv.at[i], (peer(i), a)).start()

    for i in range(1, dp_count):
        src = lax.rem(d - i + dp_count, dp_count)
        remote(col_part.at[src], col_part.at[src], c_send.at[i], c_recv.at[i], (peer(i), a)).wait_recv()
    col_sum = col_part[0]
    for i in range(1, dp_count):
        col_sum = col_sum + col_part[i]
    col_new[...] = decay * col_ref[...] + (1.0 - decay) * (col_sum * inv / D + tiny)

    for i in range(1, dp_count):
        src = lax.rem(d - i + dp_count, dp_count)
        remote(total_part.at[src], total_part.at[src], t_send.at[i], t_recv.at[i], (peer(i), a)).wait_recv()
    total = total_part[0]
    for i in range(1, dp_count):
        total = total + total_part[i]
    scale_out[...] = total / D

    @pl.loop(0, steps)
    def _(t):
        events(t, False)

    for i in range(1, dp_count):
        remote(g_ref.at[peer(i)], gt.at[a, :, tok(d)], g_send.at[i], g_recv.at[i], (peer(i), a)).wait_send()
        remote(col_part.at[d], col_part.at[d], c_send.at[i], c_recv.at[i], (peer(i), a)).wait_send()
        remote(total_part.at[d], total_part.at[d], t_send.at[i], t_recv.at[i], (peer(i), a)).wait_send()
    for j in range(1, mp_count):
        remote(gt.at[a], gt.at[a], m_send.at[j], m_recv.at[j], (d, mate(j))).wait_send()
        remote(row_part.at[a], row_part.at[a], r_send.at[j], r_recv.at[j], (d, mate(j))).wait_send()
    pltpu.make_async_copy(gt, gt_out, gt_sem).wait()

    @pl.loop(0, pieces)
    def _(c):
        pltpu.make_async_copy(hid.at[c], hid_out.at[c], out_sem.at[c]).wait()


def update_kernel(gt_ref, hid_ref, row_ref, col_ref, out_ref):
    block = hid_ref[0]
    col = col_ref[0]

    @pl.loop(0, gt_ref.shape[0])
    def _(m):
        prod = jnp.dot(gt_ref[m], block, preferred_element_type=jnp.float32)
        out_ref[m] = (prod * row_ref[m] * col).astype(jnp.bfloat16)


def body(pre_act, grad_out, row_state, col_state):
    dp_count = lax.axis_size("dp")
    mp_count = lax.axis_size("mp")
    rows, hid_cols = pre_act.shape
    tokens = rows * dp_count
    slice_width = row_state.shape[1]
    pieces = PIECES
    width = hid_cols // pieces
    f32, bf16 = jnp.float32, jnp.bfloat16
    g_blocks = grad_out.reshape(rows, dp_count, slice_width).transpose(1, 2, 0)
    whole = pl.BlockSpec(memory_space=VMEM)
    anywhere = pl.BlockSpec(memory_space=pl.ANY)
    dma = pltpu.SemaphoreType.DMA
    flops = 2 * tokens * mp_count * slice_width * hid_cols
    hid, gt, row_new, col_new, scale = pl.pallas_call(
        functools.partial(gather_kernel, dp_count, mp_count, pieces),
        out_shape=(
            jax.ShapeDtypeStruct((pieces, tokens, width), bf16),
            jax.ShapeDtypeStruct((mp_count, slice_width, tokens), bf16),
            jax.ShapeDtypeStruct((mp_count, slice_width), f32),
            jax.ShapeDtypeStruct((pieces, width), f32),
            jax.ShapeDtypeStruct((8, 128), f32),
        ),
        in_specs=[whole] * 4,
        out_specs=(anywhere, anywhere, whole, whole, whole),
        scratch_shapes=[
            VMEM((pieces, tokens, width), bf16),
            VMEM((mp_count, slice_width, tokens), bf16),
            VMEM((mp_count, slice_width, 128), f32),
            VMEM((mp_count, mp_count, slice_width), f32),
            VMEM((dp_count, pieces, width), f32),
            VMEM((dp_count, 8, 128), f32),
            dma((dp_count, pieces)), dma((dp_count, pieces)), dma((dp_count, pieces)), dma((dp_count, pieces)),
            dma, dma((dp_count,)), dma((dp_count,)), dma((mp_count,)), dma((mp_count,)),
            dma((pieces,)), dma, dma((mp_count,)), dma((mp_count,)),
            dma((dp_count,)), dma((dp_count,)), dma((dp_count,)), dma((dp_count,)),
        ],
        compiler_params=pltpu.CompilerParams(
            collective_id=0, has_side_effects=True, vmem_limit_bytes=56 * 2**20
        ),
        cost_estimate=pl.CostEstimate(
            flops=flops, bytes_accessed=2 * tokens * hid_cols * 2, transcendentals=rows * hid_cols
        ),
    )(pre_act, g_blocks, row_state, col_state.reshape(pieces, width))
    row_factor = lax.rsqrt(row_new / scale[0, 0]) / tokens
    col_factor = lax.rsqrt(col_new)
    update = pl.pallas_call(
        update_kernel,
        grid=(pieces,),
        out_shape=jax.ShapeDtypeStruct((mp_count, slice_width, hid_cols), bf16),
        in_specs=[
            pl.BlockSpec((mp_count, slice_width, tokens), lambda i: (0, 0, 0)),
            pl.BlockSpec((1, tokens, width), lambda i: (i, 0, 0)),
            pl.BlockSpec((mp_count, slice_width, 1), lambda i: (0, 0, 0)),
            pl.BlockSpec((1, 1, width), lambda i: (i, 0, 0)),
        ],
        out_specs=pl.BlockSpec((mp_count, slice_width, width), lambda i: (0, 0, i)),
        compiler_params=pltpu.CompilerParams(vmem_limit_bytes=56 * 2**20),
        cost_estimate=pl.CostEstimate(
            flops=flops, bytes_accessed=2 * (tokens + mp_count * slice_width) * hid_cols, transcendentals=0
        ),
    )(gt, hid, row_factor[:, :, None], col_factor[:, None, :])
    return update, row_new, col_new.reshape(hid_cols)


def solution(mesh):
    return jax.shard_map(
        body,
        mesh=mesh,
        in_specs=(P("dp", "mp"), P("dp", "mp"), P(None, "dp"), P("mp")),
        out_specs=(P(None, "dp", "mp"), P(None, "dp"), P("mp")),
        check_vma=False,
    )
```

```python
import functools

import jax
import jax.numpy as jnp
from jax import lax
from jax.experimental import pallas as pl
from jax.experimental.pallas import tpu as pltpu
from jax.sharding import PartitionSpec as P

D = 18432
MESH = pl.DeviceIdType.MESH
VMEM = pltpu.VMEM

decay = 1.0 - 2.0 ** (-0.8)
tiny = 1e-30

MIN_PIECES = 18
SKEW = 2
G_SEND_STEP = 4
G_READY_STEP = 16


def gather_kernel(
    dp_count, mp_count, pieces,
    pre_ref, g_ref, row_ref, col_ref,
    hid_out, gt_out, kept_out, row_new, col_new, scale_out,
    hid, gt, kept, row_acc, row_part, col_part, total_part,
    up_sem, down_sem, side_sem, recv_sem,
    g_local, g_send, g_recv, m_send, m_recv,
    out_sem, kept_sem, gt_sem, r_send, r_recv, c_send, c_recv, t_send, t_recv,
):
    rows = pre_ref.shape[0]
    width = hid.shape[2]
    depth = dp_count // 2
    slice_width = gt.shape[1]
    tokens = rows * dp_count
    d = lax.axis_index("dp")
    a = lax.axis_index("mp")
    z = d // 2
    y = d % 2
    period = 2 * max(depth - 1, 1)

    def peer(i):
        return lax.rem(d + i, dp_count)

    def mate(j):
        return lax.rem(a + j, mp_count)

    barrier = pltpu.get_barrier_semaphore()
    for i in range(1, dp_count):
        pl.semaphore_signal(barrier, inc=1, device_id=(peer(i), a), device_id_type=MESH)
    for j in range(1, mp_count):
        pl.semaphore_signal(barrier, inc=1, device_id=(d, mate(j)), device_id_type=MESH)
    pl.semaphore_wait(barrier, dp_count + mp_count - 2)

    def remote(src, dst, send, recv, device):
        return pltpu.make_async_remote_copy(
            src_ref=src, dst_ref=dst, send_sem=send, recv_sem=recv,
            device_id=device, device_id_type=MESH,
        )

    def tok(dev):
        return pl.ds(pl.multiple_of(dev * rows, rows), rows)

    own_g = pltpu.make_async_copy(g_ref.at[d], gt.at[a, :, tok(d)], g_local)
    own_g.start()
    for i in range(1, dp_count):
        remote(g_ref.at[peer(i)], gt.at[a, :, tok(d)], g_send.at[i], g_recv.at[i], (peer(i), a)).start()

    def spread_g():
        own_g.wait()
        for i in range(1, dp_count):
            src = lax.rem(d - i + dp_count, dp_count)
            block = gt.at[a, :, tok(src)]
            remote(block, block, g_send.at[i], g_recv.at[i], (peer(i), a)).wait_recv()
        for j in range(1, mp_count):
            remote(gt.at[a], gt.at[a], m_send.at[j], m_recv.at[j], (d, mate(j))).start()

    def finish_g():
        for j in range(1, mp_count):
            src = lax.rem(a - j + mp_count, mp_count)
            remote(gt.at[src], gt.at[src], m_send.at[j], m_recv.at[j], (d, mate(j))).wait_recv()
        pltpu.make_async_copy(gt, gt_out, gt_sem).start()

    def block_of(src, p):
        return hid.at[p, tok(src)]

    def arrive(src, p):
        block = block_of(src, p)
        remote(block, block, side_sem.at[src, p], recv_sem.at[src, p], (d, a)).wait_recv()

    def side_first(p):
        return lax.rem(p, period) == min(2, period - 1)

    def push(go, src, p, up, down, side):
        block = block_of(src, p)
        for wanted, sem, dev in ((up, up_sem, d + 2), (down, down_sem, d - 2), (side, side_sem, z * 2 + 1 - y)):
            if wanted is None:
                continue

            @pl.when(wanted)
            def _(sem=sem, dev=dev):
                copy = remote(block, block, sem.at[src, p], recv_sem.at[src, p], (dev, a))
                if go:
                    copy.start()
                else:
                    copy.wait_send()

    up_ok = z + 1 < depth
    down_ok = z > 0
    always = z >= 0

    def events(t, go):
        @pl.when(t < pieces)
        def _():
            if go:
                cols = pl.ds(pl.multiple_of(t * width, width), width)
                part = jax.nn.gelu(pre_ref[:, cols].astype(jnp.float32)).astype(jnp.bfloat16)
                hid[t, tok(d), :] = part
            push(go, d, t, up_ok, down_ok, always)

        def passing(zs, ys, p, valid, up, down, side):
            @pl.when(valid)
            def _():
                src = zs * 2 + ys
                if go:
                    arrive(src, p)
                push(go, src, p, up, down, side)

        for k in range(1, depth):
            p = t - SKEW * k
            live = (p >= 0) & (p < pieces)
            row_first = jnp.logical_not(side_first(p))
            passing(z - k, y, p, live & (z - k >= 0), up_ok, None, row_first)
            passing(z + k, y, p, live & (z + k < depth), None, down_ok, row_first)
        for k in range(depth):
            p = t - SKEW * (k + 1)
            live = (p >= 0) & (p < pieces) & side_first(p)
            if k == 0:
                passing(z, 1 - y, p, live, up_ok, down_ok, None)
            else:
                passing(z - k, 1 - y, p, live & (z - k >= 0), up_ok, None, None)
                passing(z + k, 1 - y, p, live & (z + k < depth), None, down_ok, None)

    row_acc[...] = jnp.zeros_like(row_acc)

    def keep(half):
        slot = lax.rem(half, 2)
        return pltpu.make_async_copy(kept.at[slot], kept_out.at[half], kept_sem.at[slot])

    def work(c):
        @pl.when(jnp.logical_not(side_first(c)))
        def _():
            for zs in range(depth):
                arrive(zs * 2 + 1 - y, c)

        half = c // 2
        even = lax.rem(c, 2) == 0
        slot = jnp.where(even, lax.rem(half, 2), 2)

        @pl.when(jnp.logical_not(even))
        def _():
            pltpu.make_async_copy(hid.at[c], hid_out.at[half], out_sem.at[half]).start()

        @pl.when(even & (half >= 2))
        def _():
            keep(half - 2).wait()

        block = hid[c]

        def one(m, col):
            prod = jnp.dot(gt[m], block, preferred_element_type=jnp.float32)
            kept[slot, m] = prod
            sq = prod * prod
            part = sq[:, 0:128]
            for q in range(1, width // 128):
                part = part + sq[:, q * 128:(q + 1) * 128]
            row_acc[m] += part
            return col + jnp.sum(sq, axis=0, keepdims=True)

        col = lax.fori_loop(0, mp_count, one, jnp.zeros((1, width), jnp.float32))
        col_part[d, pl.ds(c, 1), :] = col

        @pl.when(even)
        def _():
            keep(half).start()

    def done_by(t):
        return jnp.clip(jnp.minimum(2 * (t - G_READY_STEP + 1), t - SKEW * depth + 1), 0, pieces)

    steps = pieces + SKEW * depth

    @pl.loop(0, steps)
    def _(t):
        events(t, True)

        @pl.when(t == G_SEND_STEP)
        def _():
            spread_g()

        @pl.when(t == G_READY_STEP)
        def _():
            finish_g()

        @pl.loop(done_by(t - 1), done_by(t))
        def _(c):
            work(c)

    ones = jnp.ones((8, 128), jnp.float32)
    for m in range(mp_count):
        turned = lax.dot_general(
            ones, row_acc[m], (((1,), (1,)), ((), ())),
            precision=lax.Precision.HIGHEST, preferred_element_type=jnp.float32,
        )
        row_part[a, m:m + 1, :] = turned[0:1]
    for j in range(1, mp_count):
        remote(row_part.at[a], row_part.at[a], r_send.at[j], r_recv.at[j], (d, mate(j))).start()
    for i in range(1, dp_count):
        remote(col_part.at[d], col_part.at[d], c_send.at[i], c_recv.at[i], (peer(i), a)).start()

    for j in range(1, mp_count):
        src = lax.rem(a - j + mp_count, mp_count)
        remote(row_part.at[src], row_part.at[src], r_send.at[j], r_recv.at[j], (d, mate(j))).wait_recv()
    inv = 1.0 / (tokens * tokens)
    all_hidden = pieces * width * mp_count
    row_sum = row_part[0]
    for m in range(1, mp_count):
        row_sum = row_sum + row_part[m]
    new = decay * row_ref[...] + (1.0 - decay) * (row_sum * inv / all_hidden + tiny)
    row_new[...] = new
    own_total = jnp.sum(jnp.sum(new, axis=1, keepdims=True), axis=0, keepdims=True)
    total_part[d] = jnp.broadcast_to(own_total, (8, 128))
    for i in range(1, dp_count):
        remote(total_part.at[d], total_part.at[d], t_send.at[i], t_recv.at[i], (peer(i), a)).start()

    for i in range(1, dp_count):
        src = lax.rem(d - i + dp_count, dp_count)
        remote(col_part.at[src], col_part.at[src], c_send.at[i], c_recv.at[i], (peer(i), a)).wait_recv()
    col_sum = col_part[0]
    for i in range(1, dp_count):
        col_sum = col_sum + col_part[i]
    col_new[...] = decay * col_ref[...] + (1.0 - decay) * (col_sum * inv / D + tiny)

    for i in range(1, dp_count):
        src = lax.rem(d - i + dp_count, dp_count)
        remote(total_part.at[src], total_part.at[src], t_send.at[i], t_recv.at[i], (peer(i), a)).wait_recv()
    total = total_part[0]
    for i in range(1, dp_count):
        total = total + total_part[i]
    scale_out[...] = total / D

    @pl.loop(0, steps)
    def _(t):
        events(t, False)

    for i in range(1, dp_count):
        remote(g_ref.at[peer(i)], gt.at[a, :, tok(d)], g_send.at[i], g_recv.at[i], (peer(i), a)).wait_send()
        remote(col_part.at[d], col_part.at[d], c_send.at[i], c_recv.at[i], (peer(i), a)).wait_send()
        remote(total_part.at[d], total_part.at[d], t_send.at[i], t_recv.at[i], (peer(i), a)).wait_send()
    for j in range(1, mp_count):
        remote(gt.at[a], gt.at[a], m_send.at[j], m_recv.at[j], (d, mate(j))).wait_send()
        remote(row_part.at[a], row_part.at[a], r_send.at[j], r_recv.at[j], (d, mate(j))).wait_send()
    pltpu.make_async_copy(gt, gt_out, gt_sem).wait()

    keep(pieces // 2 - 2).wait()
    keep(pieces // 2 - 1).wait()

    @pl.loop(0, pieces // 2)
    def _(c):
        pltpu.make_async_copy(hid.at[2 * c + 1], hid_out.at[c], out_sem.at[c]).wait()


def update_kernel(tokens, gt_ref, hid_ref, kept_ref, row_ref, col_ref, scale_ref, out_ref, factor):
    i = pl.program_id(0)
    width = hid_ref.shape[2]

    @pl.when(i == 0)
    def _():
        row = lax.rsqrt(row_ref[...] / scale_ref[0:1, 0:1]) / tokens
        for m in range(row_ref.shape[0]):
            factor[m] = jnp.broadcast_to(row[m:m + 1], (128, row.shape[1])).T

    block = hid_ref[0]
    left = lax.rsqrt(col_ref[pl.ds(2 * i, 1), :])
    right = lax.rsqrt(col_ref[pl.ds(2 * i + 1, 1), :])

    @pl.loop(0, gt_ref.shape[0])
    def _(m):
        row = jnp.concatenate([factor[m]] * (width // 128), axis=1)
        prod = jnp.dot(gt_ref[m], block, preferred_element_type=jnp.float32)
        out_ref[m, :, 0:width] = (kept_ref[0, m] * row * left).astype(jnp.bfloat16)
        out_ref[m, :, width:2 * width] = (prod * row * right).astype(jnp.bfloat16)


def body(pre_act, grad_out, row_state, col_state):
    dp_count = lax.axis_size("dp")
    mp_count = lax.axis_size("mp")
    rows, hid_cols = pre_act.shape
    tokens = rows * dp_count
    slice_width = row_state.shape[1]
    width = 256 if hid_cols % 512 == 0 and hid_cols // 256 >= MIN_PIECES else 128
    pieces = hid_cols // width
    f32, bf16 = jnp.float32, jnp.bfloat16
    g_blocks = grad_out.reshape(rows, dp_count, slice_width).transpose(1, 2, 0)
    whole = pl.BlockSpec(memory_space=VMEM)
    anywhere = pl.BlockSpec(memory_space=pl.ANY)
    dma = pltpu.SemaphoreType.DMA
    flops = 2 * tokens * mp_count * slice_width * hid_cols
    hid, gt, kept, row_new, col_new, scale = pl.pallas_call(
        functools.partial(gather_kernel, dp_count, mp_count, pieces),
        out_shape=(
            jax.ShapeDtypeStruct((pieces // 2, tokens, width), bf16),
            jax.ShapeDtypeStruct((mp_count, slice_width, tokens), bf16),
            jax.ShapeDtypeStruct((pieces // 2, mp_count, slice_width, width), f32),
            jax.ShapeDtypeStruct((mp_count, slice_width), f32),
            jax.ShapeDtypeStruct((pieces, width), f32),
            jax.ShapeDtypeStruct((8, 128), f32),
        ),
        in_specs=[whole] * 4,
        out_specs=(anywhere, anywhere, anywhere, whole, whole, whole),
        scratch_shapes=[
            VMEM((pieces, tokens, width), bf16),
            VMEM((mp_count, slice_width, tokens), bf16),
            VMEM((3, mp_count, slice_width, width), f32),
            VMEM((mp_count, slice_width, 128), f32),
            VMEM((mp_count, mp_count, slice_width), f32),
            VMEM((dp_count, pieces, width), f32),
            VMEM((dp_count, 8, 128), f32),
            dma((dp_count, pieces)), dma((dp_count, pieces)), dma((dp_count, pieces)), dma((dp_count, pieces)),
            dma, dma((dp_count,)), dma((dp_count,)), dma((mp_count,)), dma((mp_count,)),
            dma((pieces // 2,)), dma((2,)), dma, dma((mp_count,)), dma((mp_count,)),
            dma((dp_count,)), dma((dp_count,)), dma((dp_count,)), dma((dp_count,)),
        ],
        compiler_params=pltpu.CompilerParams(
            collective_id=0, has_side_effects=True, vmem_limit_bytes=56 * 2**20
        ),
        cost_estimate=pl.CostEstimate(
            flops=flops, bytes_accessed=2 * tokens * hid_cols * 2, transcendentals=rows * hid_cols
        ),
    )(pre_act, g_blocks, row_state, col_state.reshape(pieces, width))
    update = pl.pallas_call(
        functools.partial(update_kernel, tokens),
        grid=(pieces // 2,),
        out_shape=jax.ShapeDtypeStruct((mp_count, slice_width, hid_cols), bf16),
        in_specs=[
            pl.BlockSpec((mp_count, slice_width, tokens), lambda i: (0, 0, 0)),
            pl.BlockSpec((1, tokens, width), lambda i: (i, 0, 0)),
            pl.BlockSpec((1, mp_count, slice_width, width), lambda i: (i, 0, 0, 0)),
            pl.BlockSpec((mp_count, slice_width), lambda i: (0, 0)),
            pl.BlockSpec((pieces, width), lambda i: (0, 0)),
            pl.BlockSpec((8, 128), lambda i: (0, 0)),
        ],
        out_specs=pl.BlockSpec((mp_count, slice_width, 2 * width), lambda i: (0, 0, i)),
        scratch_shapes=[VMEM((mp_count, slice_width, 128), f32)],
        compiler_params=pltpu.CompilerParams(vmem_limit_bytes=56 * 2**20),
        cost_estimate=pl.CostEstimate(
            flops=flops // 2, bytes_accessed=(tokens + 4 * mp_count * slice_width) * hid_cols, transcendentals=0
        ),
    )(gt, hid, kept, row_new, col_new, scale)
    return update, row_new, col_new.reshape(hid_cols)


def solution(mesh):
    return jax.shard_map(
        body,
        mesh=mesh,
        in_specs=(P("dp", "mp"), P("dp", "mp"), P(None, "dp"), P("mp")),
        out_specs=(P(None, "dp", "mp"), P(None, "dp"), P("mp")),
        check_vma=False,
    )
```

```python
import functools

import jax
import jax.numpy as jnp
from jax import lax
from jax.experimental import pallas as pl
from jax.experimental.pallas import tpu as pltpu
from jax.sharding import PartitionSpec as P

D = 18432
MESH = pl.DeviceIdType.MESH
VMEM = pltpu.VMEM

decay = 1.0 - 2.0 ** (-0.8)
tiny = 1e-30

MIN_PIECES = 18
SKEW = 2
DRAIN_LAG = 6
G_SEND_STEP = 4
G_READY_STEP = 16


def gather_kernel(
    dp_count, mp_count, pieces,
    pre_ref, g_ref, row_ref, col_ref,
    hid_out, gt_out, kept_out, row_new, col_new, scale_out,
    hid, gt, kept, row_acc, row_part, col_part, total_part,
    up_sem, down_sem, side_sem, recv_sem,
    g_local, g_send, g_recv, m_send, m_recv,
    out_sem, kept_sem, gt_sem, r_send, r_recv, c_send, c_recv, t_send, t_recv,
):
    rows = pre_ref.shape[0]
    width = hid.shape[2]
    depth = dp_count // 2
    slice_width = gt.shape[1]
    tokens = rows * dp_count
    d = lax.axis_index("dp")
    a = lax.axis_index("mp")
    z = d // 2
    y = d % 2
    period = 2 * max(depth, 1)

    def peer(i):
        return lax.rem(d + i, dp_count)

    def mate(j):
        return lax.rem(a + j, mp_count)

    barrier = pltpu.get_barrier_semaphore()
    for i in range(1, dp_count):
        pl.semaphore_signal(barrier, inc=1, device_id=(peer(i), a), device_id_type=MESH)
    for j in range(1, mp_count):
        pl.semaphore_signal(barrier, inc=1, device_id=(d, mate(j)), device_id_type=MESH)
    pl.semaphore_wait(barrier, dp_count + mp_count - 2)

    def remote(src, dst, send, recv, device):
        return pltpu.make_async_remote_copy(
            src_ref=src, dst_ref=dst, send_sem=send, recv_sem=recv,
            device_id=device, device_id_type=MESH,
        )

    def tok(dev):
        return pl.ds(pl.multiple_of(dev * rows, rows), rows)

    own_g = pltpu.make_async_copy(g_ref.at[d], gt.at[a, :, tok(d)], g_local)
    own_g.start()
    for i in range(1, dp_count):
        remote(g_ref.at[peer(i)], gt.at[a, :, tok(d)], g_send.at[i], g_recv.at[i], (peer(i), a)).start()

    def spread_g():
        own_g.wait()
        for i in range(1, dp_count):
            src = lax.rem(d - i + dp_count, dp_count)
            block = gt.at[a, :, tok(src)]
            remote(block, block, g_send.at[i], g_recv.at[i], (peer(i), a)).wait_recv()
        for j in range(1, mp_count):
            remote(gt.at[a], gt.at[a], m_send.at[j], m_recv.at[j], (d, mate(j))).start()

    def finish_g():
        for j in range(1, mp_count):
            src = lax.rem(a - j + mp_count, mp_count)
            remote(gt.at[src], gt.at[src], m_send.at[j], m_recv.at[j], (d, mate(j))).wait_recv()
        pltpu.make_async_copy(gt, gt_out, gt_sem).start()

    def block_of(src, p):
        return hid.at[p, tok(src)]

    def arrive(src, p):
        block = block_of(src, p)
        remote(block, block, side_sem.at[src, p], recv_sem.at[src, p], (d, a)).wait_recv()

    def side_first(p):
        return lax.rem(p, period) == min(4, period - 1)

    def push(go, src, p, up, down, side):
        block = block_of(src, p)
        for wanted, sem, dev in ((up, up_sem, d + 2), (down, down_sem, d - 2), (side, side_sem, z * 2 + 1 - y)):
            if wanted is None:
                continue

            @pl.when(wanted)
            def _(sem=sem, dev=dev):
                copy = remote(block, block, sem.at[src, p], recv_sem.at[src, p], (dev, a))
                if go:
                    copy.start()
                else:
                    copy.wait_send()

    up_ok = z + 1 < depth
    down_ok = z > 0
    always = z >= 0

    def events(t, go):
        @pl.when(t < pieces)
        def _():
            if go:
                cols = pl.ds(pl.multiple_of(t * width, width), width)
                part = jax.nn.gelu(pre_ref[:, cols].astype(jnp.float32)).astype(jnp.bfloat16)
                hid[t, tok(d), :] = part
            push(go, d, t, up_ok, down_ok, always)

        def passing(zs, ys, p, valid, up, down, side):
            @pl.when(valid)
            def _():
                src = zs * 2 + ys
                if go:
                    arrive(src, p)
                push(go, src, p, up, down, side)

        for k in range(1, depth):
            p = t - SKEW * k
            live = (p >= 0) & (p < pieces)
            row_first = jnp.logical_not(side_first(p))
            passing(z - k, y, p, live & (z - k >= 0), up_ok, None, row_first)
            passing(z + k, y, p, live & (z + k < depth), None, down_ok, row_first)
        for k in range(depth):
            p = t - SKEW * (k + 1)
            live = (p >= 0) & (p < pieces) & side_first(p)
            if k == 0:
                passing(z, 1 - y, p, live, up_ok, down_ok, None)
            else:
                passing(z - k, 1 - y, p, live & (z - k >= 0), up_ok, None, None)
                passing(z + k, 1 - y, p, live & (z + k < depth), None, down_ok, None)

    row_acc[...] = jnp.zeros_like(row_acc)

    def keep(half):
        slot = lax.rem(half, 2)
        return pltpu.make_async_copy(kept.at[slot], kept_out.at[half], kept_sem.at[slot])

    def work(c):
        @pl.when(jnp.logical_not(side_first(c)))
        def _():
            for zs in range(depth):
                arrive(zs * 2 + 1 - y, c)

        half = c // 2
        even = lax.rem(c, 2) == 0
        slot = jnp.where(even, lax.rem(half, 2), 2)

        @pl.when(jnp.logical_not(even))
        def _():
            pltpu.make_async_copy(hid.at[c], hid_out.at[half], out_sem.at[half]).start()

        @pl.when(even & (half >= 2))
        def _():
            keep(half - 2).wait()

        block = hid[c]

        def one(m, col):
            prod = jnp.dot(gt[m], block, preferred_element_type=jnp.float32)
            kept[slot, m] = prod
            sq = prod * prod
            part = sq[:, 0:128]
            for q in range(1, width // 128):
                part = part + sq[:, q * 128:(q + 1) * 128]
            row_acc[m] += part
            return col + jnp.sum(sq, axis=0, keepdims=True)

        col = lax.fori_loop(0, mp_count, one, jnp.zeros((1, width), jnp.float32))
        col_part[d, pl.ds(c, 1), :] = col

        @pl.when(even)
        def _():
            keep(half).start()

    def done_by(t):
        return jnp.clip(jnp.minimum(2 * (t - G_READY_STEP + 1), t - SKEW * depth + 1), 0, pieces)

    steps = pieces + SKEW * depth

    @pl.loop(0, steps)
    def _(t):
        events(t, True)

        @pl.when(t >= DRAIN_LAG)
        def _():
            events(t - DRAIN_LAG, False)

        @pl.when(t == G_SEND_STEP)
        def _():
            spread_g()

        @pl.when(t == G_READY_STEP)
        def _():
            finish_g()

        @pl.loop(done_by(t - 1), done_by(t))
        def _(c):
            work(c)

    ones = jnp.ones((8, 128), jnp.float32)
    for m in range(mp_count):
        turned = lax.dot_general(
            ones, row_acc[m], (((1,), (1,)), ((), ())),
            precision=lax.Precision.HIGHEST, preferred_element_type=jnp.float32,
        )
        row_part[a, m:m + 1, :] = turned[0:1]
    for j in range(1, mp_count):
        remote(row_part.at[a], row_part.at[a], r_send.at[j], r_recv.at[j], (d, mate(j))).start()
    for i in range(1, dp_count):
        remote(col_part.at[d], col_part.at[d], c_send.at[i], c_recv.at[i], (peer(i), a)).start()

    @pl.loop(steps - DRAIN_LAG, steps)
    def _(t):
        events(t, False)

    for j in range(1, mp_count):
        src = lax.rem(a - j + mp_count, mp_count)
        remote(row_part.at[src], row_part.at[src], r_send.at[j], r_recv.at[j], (d, mate(j))).wait_recv()
    inv = 1.0 / (tokens * tokens)
    all_hidden = pieces * width * mp_count
    row_sum = row_part[0]
    for m in range(1, mp_count):
        row_sum = row_sum + row_part[m]
    new = decay * row_ref[...] + (1.0 - decay) * (row_sum * inv / all_hidden + tiny)
    row_new[...] = new
    own_total = jnp.sum(jnp.sum(new, axis=1, keepdims=True), axis=0, keepdims=True)
    total_part[d] = jnp.broadcast_to(own_total, (8, 128))
    for i in range(1, dp_count):
        remote(total_part.at[d], total_part.at[d], t_send.at[i], t_recv.at[i], (peer(i), a)).start()

    for i in range(1, dp_count):
        src = lax.rem(d - i + dp_count, dp_count)
        remote(col_part.at[src], col_part.at[src], c_send.at[i], c_recv.at[i], (peer(i), a)).wait_recv()
    col_sum = col_part[0]
    for i in range(1, dp_count):
        col_sum = col_sum + col_part[i]
    col_new[...] = decay * col_ref[...] + (1.0 - decay) * (col_sum * inv / D + tiny)

    for i in range(1, dp_count):
        src = lax.rem(d - i + dp_count, dp_count)
        remote(total_part.at[src], total_part.at[src], t_send.at[i], t_recv.at[i], (peer(i), a)).wait_recv()
    total = total_part[0]
    for i in range(1, dp_count):
        total = total + total_part[i]
    scale_out[...] = total / D

    for i in range(1, dp_count):
        remote(g_ref.at[peer(i)], gt.at[a, :, tok(d)], g_send.at[i], g_recv.at[i], (peer(i), a)).wait_send()
        remote(col_part.at[d], col_part.at[d], c_send.at[i], c_recv.at[i], (peer(i), a)).wait_send()
        remote(total_part.at[d], total_part.at[d], t_send.at[i], t_recv.at[i], (peer(i), a)).wait_send()
    for j in range(1, mp_count):
        remote(gt.at[a], gt.at[a], m_send.at[j], m_recv.at[j], (d, mate(j))).wait_send()
        remote(row_part.at[a], row_part.at[a], r_send.at[j], r_recv.at[j], (d, mate(j))).wait_send()
    pltpu.make_async_copy(gt, gt_out, gt_sem).wait()

    keep(pieces // 2 - 2).wait()
    keep(pieces // 2 - 1).wait()

    @pl.loop(0, pieces // 2)
    def _(c):
        pltpu.make_async_copy(hid.at[2 * c + 1], hid_out.at[c], out_sem.at[c]).wait()


def update_kernel(tokens, gt_ref, hid_ref, kept_ref, row_ref, col_ref, scale_ref, out_ref, factor):
    i = pl.program_id(0)
    width = hid_ref.shape[2]

    @pl.when(i == 0)
    def _():
        row = lax.rsqrt(row_ref[...] / scale_ref[0:1, 0:1]) / tokens
        for m in range(row_ref.shape[0]):
            factor[m] = jnp.broadcast_to(row[m:m + 1], (128, row.shape[1])).T

    block = hid_ref[0]
    left = lax.rsqrt(col_ref[pl.ds(2 * i, 1), :])
    right = lax.rsqrt(col_ref[pl.ds(2 * i + 1, 1), :])

    prod = jnp.dot(gt_ref[...], block, preferred_element_type=jnp.float32)
    count, slice_width = row_ref.shape
    for m in range(count):
        row = jnp.concatenate([factor[m]] * (width // 128), axis=1)
        part = prod[m * slice_width:(m + 1) * slice_width]
        out_ref[m, :, 0:width] = (kept_ref[0, m] * row * left).astype(jnp.bfloat16)
        out_ref[m, :, width:2 * width] = (part * row * right).astype(jnp.bfloat16)


def body(pre_act, grad_out, row_state, col_state):
    dp_count = lax.axis_size("dp")
    mp_count = lax.axis_size("mp")
    rows, hid_cols = pre_act.shape
    tokens = rows * dp_count
    slice_width = row_state.shape[1]
    width = 256 if hid_cols % 512 == 0 and hid_cols // 256 >= MIN_PIECES else 128
    pieces = hid_cols // width
    f32, bf16 = jnp.float32, jnp.bfloat16
    g_blocks = grad_out.reshape(rows, dp_count, slice_width).transpose(1, 2, 0)
    whole = pl.BlockSpec(memory_space=VMEM)
    anywhere = pl.BlockSpec(memory_space=pl.ANY)
    dma = pltpu.SemaphoreType.DMA
    flops = 2 * tokens * mp_count * slice_width * hid_cols
    hid, gt, kept, row_new, col_new, scale = pl.pallas_call(
        functools.partial(gather_kernel, dp_count, mp_count, pieces),
        out_shape=(
            jax.ShapeDtypeStruct((pieces // 2, tokens, width), bf16),
            jax.ShapeDtypeStruct((mp_count, slice_width, tokens), bf16),
            jax.ShapeDtypeStruct((pieces // 2, mp_count, slice_width, width), f32),
            jax.ShapeDtypeStruct((mp_count, slice_width), f32),
            jax.ShapeDtypeStruct((pieces, width), f32),
            jax.ShapeDtypeStruct((8, 128), f32),
        ),
        in_specs=[whole] * 4,
        out_specs=(anywhere, anywhere, anywhere, whole, whole, whole),
        scratch_shapes=[
            VMEM((pieces, tokens, width), bf16),
            VMEM((mp_count, slice_width, tokens), bf16),
            VMEM((3, mp_count, slice_width, width), f32),
            VMEM((mp_count, slice_width, 128), f32),
            VMEM((mp_count, mp_count, slice_width), f32),
            VMEM((dp_count, pieces, width), f32),
            VMEM((dp_count, 8, 128), f32),
            dma((dp_count, pieces)), dma((dp_count, pieces)), dma((dp_count, pieces)), dma((dp_count, pieces)),
            dma, dma((dp_count,)), dma((dp_count,)), dma((mp_count,)), dma((mp_count,)),
            dma((pieces // 2,)), dma((2,)), dma, dma((mp_count,)), dma((mp_count,)),
            dma((dp_count,)), dma((dp_count,)), dma((dp_count,)), dma((dp_count,)),
        ],
        compiler_params=pltpu.CompilerParams(
            collective_id=0, has_side_effects=True, vmem_limit_bytes=56 * 2**20
        ),
        cost_estimate=pl.CostEstimate(
            flops=flops, bytes_accessed=2 * tokens * hid_cols * 2, transcendentals=rows * hid_cols
        ),
    )(pre_act, g_blocks, row_state, col_state.reshape(pieces, width))
    update = pl.pallas_call(
        functools.partial(update_kernel, tokens),
        grid=(pieces // 2,),
        out_shape=jax.ShapeDtypeStruct((mp_count, slice_width, hid_cols), bf16),
        in_specs=[
            pl.BlockSpec((mp_count * slice_width, tokens), lambda i: (0, 0)),
            pl.BlockSpec((1, tokens, width), lambda i: (i, 0, 0)),
            pl.BlockSpec((1, mp_count, slice_width, width), lambda i: (i, 0, 0, 0)),
            pl.BlockSpec((mp_count, slice_width), lambda i: (0, 0)),
            pl.BlockSpec((pieces, width), lambda i: (0, 0)),
            pl.BlockSpec((8, 128), lambda i: (0, 0)),
        ],
        out_specs=pl.BlockSpec((mp_count, slice_width, 2 * width), lambda i: (0, 0, i)),
        scratch_shapes=[VMEM((mp_count, slice_width, 128), f32)],
        compiler_params=pltpu.CompilerParams(vmem_limit_bytes=56 * 2**20),
        cost_estimate=pl.CostEstimate(
            flops=flops // 2, bytes_accessed=(tokens + 4 * mp_count * slice_width) * hid_cols, transcendentals=0
        ),
    )(gt.reshape(mp_count * slice_width, tokens), hid, kept, row_new, col_new, scale)
    return update, row_new, col_new.reshape(hid_cols)


def solution(mesh):
    return jax.shard_map(
        body,
        mesh=mesh,
        in_specs=(P("dp", "mp"), P("dp", "mp"), P(None, "dp"), P("mp")),
        out_specs=(P(None, "dp", "mp"), P(None, "dp"), P("mp")),
        check_vma=False,
    )
```

```python
import functools

import jax
import jax.numpy as jnp
from jax import lax
from jax.experimental import pallas as pl
from jax.experimental.pallas import tpu as pltpu
from jax.sharding import PartitionSpec as P

D = 18432
MESH = pl.DeviceIdType.MESH
VMEM = pltpu.VMEM

decay = 1.0 - 2.0 ** (-0.8)
tiny = 1e-30

MIN_PIECES = 18
SKEW = 2
DRAIN_LAG = 6
G_SEND_STEP = 4
G_PASS_STEP = 10
G_READY_STEP = 11


def gather_kernel(
    dp_count, mp_count, pieces,
    pre_ref, g_ref, row_ref, col_ref,
    kept_out, row_new, col_new, scale_out,
    hid, gt, kept, row_acc, row_part, col_part, total_part,
    up_sem, down_sem, side_sem, recv_sem,
    g_local, g_send, g_recv, m_send, m_recv, n_send,
    kept_sem, r_send, r_recv, c_send, c_recv, t_send, t_recv,
):
    rows = pre_ref.shape[0]
    width = hid.shape[2]
    depth = dp_count // 2
    slice_width = gt.shape[1]
    tokens = rows * dp_count
    d = lax.axis_index("dp")
    a = lax.axis_index("mp")
    z = d // 2
    y = d % 2
    period = 2 * max(depth, 1)

    def peer(i):
        return lax.rem(d + i, dp_count)

    def mate(j):
        return lax.rem(a + j, mp_count)

    barrier = pltpu.get_barrier_semaphore()
    for i in range(1, dp_count):
        pl.semaphore_signal(barrier, inc=1, device_id=(peer(i), a), device_id_type=MESH)
    for j in range(1, mp_count):
        pl.semaphore_signal(barrier, inc=1, device_id=(d, mate(j)), device_id_type=MESH)
    pl.semaphore_wait(barrier, dp_count + mp_count - 2)

    def remote(src, dst, send, recv, device):
        return pltpu.make_async_remote_copy(
            src_ref=src, dst_ref=dst, send_sem=send, recv_sem=recv,
            device_id=device, device_id_type=MESH,
        )

    def tok(dev):
        return pl.ds(pl.multiple_of(dev * rows, rows), rows)

    own_g = pltpu.make_async_copy(g_ref.at[d], gt.at[a, :, tok(d)], g_local)
    own_g.start()
    for i in range(1, dp_count):
        remote(g_ref.at[peer(i)], gt.at[a, :, tok(d)], g_send.at[i], g_recv.at[i], (peer(i), a)).start()

    def spread_g():
        own_g.wait()
        for i in range(1, dp_count):
            src = lax.rem(d - i + dp_count, dp_count)
            block = gt.at[a, :, tok(src)]
            remote(block, block, g_send.at[i], g_recv.at[i], (peer(i), a)).wait_recv()
        for j in range(1, mp_count):
            send_g(j, True)

    def twin_of(m):
        return m + 1 - 2 * lax.rem(m, 2)

    twin = twin_of(a)

    def slab(m, send, dev):
        return remote(gt.at[m], gt.at[m], send, m_recv.at[m], (d, dev))

    def send_g(j, go):
        dst = mate(j)

        def act():
            copy = slab(a, m_send.at[j], dst)
            if go:
                copy.start()
            else:
                copy.wait_send()

        if j % 2 == 0:
            act()
        else:
            pl.when(dst == twin)(act)

    def pass_g():
        for j in range(2, mp_count, 2):
            src = mate(j)
            slab(src, n_send.at[j], twin).wait_recv()
            slab(src, n_send.at[j], twin).start()

    def finish_g():
        for j in range(1, mp_count, 2):
            slab(mate(j), n_send.at[j], twin).wait_recv()

    def block_of(src, p):
        return hid.at[p, tok(src)]

    def arrive(src, p):
        block = block_of(src, p)
        remote(block, block, side_sem.at[src, p], recv_sem.at[src, p], (d, a)).wait_recv()

    def side_first(p):
        return lax.rem(p, period) == min(4, period - 1)

    def push(go, src, p, up, down, side):
        block = block_of(src, p)
        for wanted, sem, dev in ((up, up_sem, d + 2), (down, down_sem, d - 2), (side, side_sem, z * 2 + 1 - y)):
            if wanted is None:
                continue

            @pl.when(wanted)
            def _(sem=sem, dev=dev):
                copy = remote(block, block, sem.at[src, p], recv_sem.at[src, p], (dev, a))
                if go:
                    copy.start()
                else:
                    copy.wait_send()

    up_ok = z + 1 < depth
    down_ok = z > 0
    always = z >= 0

    def events(t, go):
        @pl.when(t < pieces)
        def _():
            if go:
                cols = pl.ds(pl.multiple_of(t * width, width), width)
                part = jax.nn.gelu(pre_ref[:, cols].astype(jnp.float32)).astype(jnp.bfloat16)
                hid[t, tok(d), :] = part
            push(go, d, t, up_ok, down_ok, always)

        def passing(zs, ys, p, valid, up, down, side):
            @pl.when(valid)
            def _():
                src = zs * 2 + ys
                if go:
                    arrive(src, p)
                push(go, src, p, up, down, side)

        for k in range(1, depth):
            p = t - SKEW * k
            live = (p >= 0) & (p < pieces)
            row_first = jnp.logical_not(side_first(p))
            passing(z - k, y, p, live & (z - k >= 0), up_ok, None, row_first)
            passing(z + k, y, p, live & (z + k < depth), None, down_ok, row_first)
        for k in range(depth):
            p = t - SKEW * (k + 1)
            live = (p >= 0) & (p < pieces) & side_first(p)
            if k == 0:
                passing(z, 1 - y, p, live, up_ok, down_ok, None)
            else:
                passing(z - k, 1 - y, p, live & (z - k >= 0), up_ok, None, None)
                passing(z + k, 1 - y, p, live & (z + k < depth), None, down_ok, None)

    row_acc[...] = jnp.zeros_like(row_acc)

    def keep(c):
        slot = lax.rem(c, 2)
        return pltpu.make_async_copy(kept.at[slot], kept_out.at[c], kept_sem.at[slot])

    def work(c):
        @pl.when(jnp.logical_not(side_first(c)))
        def _():
            for zs in range(depth):
                arrive(zs * 2 + 1 - y, c)

        slot = lax.rem(c, 2)

        @pl.when(c >= 2)
        def _():
            keep(c - 2).wait()

        block = hid[c]

        col = jnp.zeros((1, width), jnp.float32)
        for m in range(mp_count):
            prod = jnp.dot(gt[m], block, preferred_element_type=jnp.float32)
            kept[slot, m] = prod
            sq = prod * prod
            part = sq[:, 0:128]
            for q in range(1, width // 128):
                part = part + sq[:, q * 128:(q + 1) * 128]
            row_acc[m] += part
            col = col + jnp.sum(sq, axis=0, keepdims=True)
        col_part[d, pl.ds(c, 1), :] = col
        keep(c).start()

    def done_by(t):
        return jnp.clip(jnp.minimum(2 * (t - G_READY_STEP + 1), t - SKEW * depth + 1), 0, pieces)

    steps = pieces + SKEW * depth

    @pl.loop(0, steps)
    def _(t):
        events(t, True)

        @pl.when(t >= DRAIN_LAG)
        def _():
            events(t - DRAIN_LAG, False)

        @pl.when(t == G_SEND_STEP)
        def _():
            spread_g()

        @pl.when(t == G_PASS_STEP)
        def _():
            pass_g()

        @pl.when(t == G_READY_STEP)
        def _():
            finish_g()

        @pl.loop(done_by(t - 1), done_by(t))
        def _(c):
            work(c)

    ones = jnp.ones((8, 128), jnp.float32)
    for m in range(mp_count):
        turned = lax.dot_general(
            ones, row_acc[m], (((1,), (1,)), ((), ())),
            precision=lax.Precision.HIGHEST, preferred_element_type=jnp.float32,
        )
        row_part[a, m:m + 1, :] = turned[0:1]
    for j in range(1, mp_count):
        remote(row_part.at[a], row_part.at[a], r_send.at[j], r_recv.at[j], (d, mate(j))).start()
    for i in range(1, dp_count):
        remote(col_part.at[d], col_part.at[d], c_send.at[i], c_recv.at[i], (peer(i), a)).start()

    @pl.loop(steps - DRAIN_LAG, steps)
    def _(t):
        events(t, False)

    for j in range(1, mp_count):
        src = lax.rem(a - j + mp_count, mp_count)
        remote(row_part.at[src], row_part.at[src], r_send.at[j], r_recv.at[j], (d, mate(j))).wait_recv()
    inv = 1.0 / (tokens * tokens)
    all_hidden = pieces * width * mp_count
    row_sum = row_part[0]
    for m in range(1, mp_count):
        row_sum = row_sum + row_part[m]
    new = decay * row_ref[...] + (1.0 - decay) * (row_sum * inv / all_hidden + tiny)
    row_new[...] = new
    own_total = jnp.sum(jnp.sum(new, axis=1, keepdims=True), axis=0, keepdims=True)
    total_part[d] = jnp.broadcast_to(own_total, (8, 128))
    for i in range(1, dp_count):
        remote(total_part.at[d], total_part.at[d], t_send.at[i], t_recv.at[i], (peer(i), a)).start()

    for i in range(1, dp_count):
        src = lax.rem(d - i + dp_count, dp_count)
        remote(col_part.at[src], col_part.at[src], c_send.at[i], c_recv.at[i], (peer(i), a)).wait_recv()
    col_sum = col_part[0]
    for i in range(1, dp_count):
        col_sum = col_sum + col_part[i]
    col_new[...] = decay * col_ref[...] + (1.0 - decay) * (col_sum * inv / D + tiny)

    for i in range(1, dp_count):
        src = lax.rem(d - i + dp_count, dp_count)
        remote(total_part.at[src], total_part.at[src], t_send.at[i], t_recv.at[i], (peer(i), a)).wait_recv()
    total = total_part[0]
    for i in range(1, dp_count):
        total = total + total_part[i]
    scale_out[...] = total / D

    for i in range(1, dp_count):
        remote(g_ref.at[peer(i)], gt.at[a, :, tok(d)], g_send.at[i], g_recv.at[i], (peer(i), a)).wait_send()
        remote(col_part.at[d], col_part.at[d], c_send.at[i], c_recv.at[i], (peer(i), a)).wait_send()
        remote(total_part.at[d], total_part.at[d], t_send.at[i], t_recv.at[i], (peer(i), a)).wait_send()
    for j in range(1, mp_count):
        send_g(j, False)
        if j % 2 == 0:
            slab(mate(j), n_send.at[j], twin).wait_send()
        remote(row_part.at[a], row_part.at[a], r_send.at[j], r_recv.at[j], (d, mate(j))).wait_send()
    keep(pieces - 2).wait()
    keep(pieces - 1).wait()


def update_kernel(tokens, kept_ref, row_ref, col_ref, scale_ref, out_ref, factor):
    i = pl.program_id(0)
    count, width = kept_ref.shape[0], kept_ref.shape[3]

    @pl.when(i == 0)
    def _():
        row = lax.rsqrt(row_ref[...] / scale_ref[0:1, 0:1]) / tokens
        for m in range(row_ref.shape[0]):
            factor[m] = jnp.broadcast_to(row[m:m + 1], (128, row.shape[1])).T

    cols = [lax.rsqrt(col_ref[pl.ds(count * i + n, 1), :]) for n in range(count)]

    @pl.loop(0, row_ref.shape[0])
    def _(m):
        row = jnp.concatenate([factor[m]] * (width // 128), axis=1)
        for n in range(count):
            out_ref[m, :, n * width:(n + 1) * width] = (kept_ref[n, m] * row * cols[n]).astype(jnp.bfloat16)


def body(pre_act, grad_out, row_state, col_state):
    dp_count = lax.axis_size("dp")
    mp_count = lax.axis_size("mp")
    rows, hid_cols = pre_act.shape
    tokens = rows * dp_count
    slice_width = row_state.shape[1]
    width = 256 if hid_cols % 512 == 0 and hid_cols // 256 >= MIN_PIECES else 128
    pieces = hid_cols // width
    f32, bf16 = jnp.float32, jnp.bfloat16
    g_blocks = grad_out.reshape(rows, dp_count, slice_width).transpose(1, 2, 0)
    whole = pl.BlockSpec(memory_space=VMEM)
    anywhere = pl.BlockSpec(memory_space=pl.ANY)
    dma = pltpu.SemaphoreType.DMA
    flops = 2 * tokens * mp_count * slice_width * hid_cols
    kept, row_new, col_new, scale = pl.pallas_call(
        functools.partial(gather_kernel, dp_count, mp_count, pieces),
        out_shape=(
            jax.ShapeDtypeStruct((pieces, mp_count, slice_width, width), f32),
            jax.ShapeDtypeStruct((mp_count, slice_width), f32),
            jax.ShapeDtypeStruct((pieces, width), f32),
            jax.ShapeDtypeStruct((8, 128), f32),
        ),
        in_specs=[whole] * 4,
        out_specs=(anywhere, whole, whole, whole),
        scratch_shapes=[
            VMEM((pieces, tokens, width), bf16),
            VMEM((mp_count, slice_width, tokens), bf16),
            VMEM((2, mp_count, slice_width, width), f32),
            VMEM((mp_count, slice_width, 128), f32),
            VMEM((mp_count, mp_count, slice_width), f32),
            VMEM((dp_count, pieces, width), f32),
            VMEM((dp_count, 8, 128), f32),
            dma((dp_count, pieces)), dma((dp_count, pieces)), dma((dp_count, pieces)), dma((dp_count, pieces)),
            dma, dma((dp_count,)), dma((dp_count,)), dma((mp_count,)), dma((mp_count,)), dma((mp_count,)),
            dma((2,)), dma((mp_count,)), dma((mp_count,)),
            dma((dp_count,)), dma((dp_count,)), dma((dp_count,)), dma((dp_count,)),
        ],
        compiler_params=pltpu.CompilerParams(
            collective_id=0, has_side_effects=True, vmem_limit_bytes=56 * 2**20
        ),
        cost_estimate=pl.CostEstimate(
            flops=flops, bytes_accessed=2 * tokens * hid_cols * 2, transcendentals=rows * hid_cols
        ),
    )(pre_act, g_blocks, row_state, col_state.reshape(pieces, width))
    update = pl.pallas_call(
        functools.partial(update_kernel, tokens),
        grid=(pieces // 2,),
        out_shape=jax.ShapeDtypeStruct((mp_count, slice_width, hid_cols), bf16),
        in_specs=[
            pl.BlockSpec((2, mp_count, slice_width, width), lambda i: (i, 0, 0, 0)),
            pl.BlockSpec((mp_count, slice_width), lambda i: (0, 0)),
            pl.BlockSpec((pieces, width), lambda i: (0, 0)),
            pl.BlockSpec((8, 128), lambda i: (0, 0)),
        ],
        out_specs=pl.BlockSpec((mp_count, slice_width, 2 * width), lambda i: (0, 0, i)),
        scratch_shapes=[VMEM((mp_count, slice_width, 128), f32)],
        compiler_params=pltpu.CompilerParams(vmem_limit_bytes=56 * 2**20),
        cost_estimate=pl.CostEstimate(
            flops=2 * mp_count * slice_width * hid_cols, bytes_accessed=6 * mp_count * slice_width * hid_cols, transcendentals=0
        ),
    )(kept, row_new, col_new, scale)
    return update, row_new, col_new.reshape(hid_cols)


def solution(mesh):
    return jax.shard_map(
        body,
        mesh=mesh,
        in_specs=(P("dp", "mp"), P("dp", "mp"), P(None, "dp"), P("mp")),
        out_specs=(P(None, "dp", "mp"), P(None, "dp"), P("mp")),
        check_vma=False,
    )
```
